32 devices in a mesh: grp: 2 (over x), head: 16 (over z, y, core).
Axes of the slice: x: 2, y: 2, z: 4, core: 2. Of those that a mesh axis runs over, the one named last changes fastest.
Arguments:
- query: bfloat16 [72, 256, 2048], P('grp', 'head'), may hold values from -24 to 24
- out_grad: bfloat16 [72, 256, 2048], P('grp', 'head'), may hold values from -6 to 6
- forward_out: bfloat16 [72, 256, 2048], P('grp', 'head'), may hold values from -6 to 6
- key_codes: bfloat16 [4, 256, 2048], P('grp', 'head'), may hold values from -127 to 127, as said below
- key_scale: bfloat16 [4, 256, 16], P('grp', 'head'), may hold values from 0.0039 to 0.0402
- value_codes: bfloat16 [4, 256, 2048], P('grp', 'head'), may hold values from -127 to 127, as said below
- value_scale: bfloat16 [4, 256, 16], P('grp', 'head'), may hold values from 0.0039 to 0.0402
- pairing: int32 [72, 2], replicated, may hold values from 0 to 3, as said below
Outputs:
- grad_query: bfloat16 [72, 256, 2048], P('grp', 'head')
- grad_key: bfloat16 [4, 256, 2048], P('grp', 'head')
- grad_value: bfloat16 [4, 256, 2048], P('grp', 'head')
The draws below stay inside these ranges and needn't reach their ends.
Inputs may be any that keep to these rules, and one draw needn't show every extreme that they name: `key_codes`: whole numbers. `value_codes`: whole numbers. `pairing`: the two entries of a row differ.
All inputs are finite; a program needn't handle non-finite values.
Results may differ from the reference program's by a relative error of at most 0.012.
The reference program's roundings to bfloat16 on the way (of `keys`, `values`, `key_set`, `rounded` and `score_grad`) count: a program that leaves them out, or rounds other values in their place, can miss the bound.
Values may be sent and summed in bfloat16 or wider, within the bound.
A program may use at most 192 MiB of HBM per device.

```python
import math
import jax
import jax.numpy as jnp
from jax import lax

HD = 128
H = 16
D = 2048
L = 256
QC = 72
KC = 4


def kv_tables(key):
    low = math.log(0.004)
    high = math.log(0.04)
    key_part = jax.random.randint(jax.random.fold_in(key, 101), (KC, L, D), -127, 128).astype(jnp.float32)
    key_scales = jnp.exp(jax.random.uniform(jax.random.fold_in(key, 102), (KC, L, H), minval=low, maxval=high))
    value_part = jax.random.randint(jax.random.fold_in(key, 103), (KC, L, D), -127, 128).astype(jnp.float32)
    value_scales = jnp.exp(jax.random.uniform(jax.random.fold_in(key, 104), (KC, L, H), minval=low, maxval=high))
    return (key_part, key_scales, value_part, value_scales)


def pair_table(key):
    row_keys = jax.random.split(jax.random.fold_in(key, 301), QC)
    return jax.vmap(lambda row_key: jax.random.permutation(row_key, KC)[:2])(row_keys).astype(jnp.int32)


def draw_query(key, part):
    result = jnp.clip(jax.random.normal(jax.random.fold_in(key, 201), (QC, L, D)), -6.0, 6.0)
    return result.astype(jnp.bfloat16)


def draw_key_codes(key, part):
    return kv_tables(key)[0].astype(jnp.bfloat16)


def draw_key_scale(key, part):
    return kv_tables(key)[1].astype(jnp.bfloat16)


def draw_value_codes(key, part):
    return kv_tables(key)[2].astype(jnp.bfloat16)


def draw_value_scale(key, part):
    return kv_tables(key)[3].astype(jnp.bfloat16)


def draw_pairing(key, part):
    return pair_table(key)


def levels(own_key, dims, shards, least, high):
    level, own = 1.0, jax.random.fold_in(own_key, 6)
    for axis_at, shards_of in shards:
        heights = jnp.exp(jax.random.uniform(jax.random.fold_in(own, axis_at), (shards_of,), jnp.float32, least / len(shards), high / len(shards)))
        level = level * jnp.repeat(heights, dims[axis_at] // shards_of).reshape([-1 if axis == axis_at else 1 for axis in range(len(dims))])
    return level


def normal_values(stream_key, extent, spread, reach, cuts=(), held_as=jnp.bfloat16):
    gain = levels(stream_key, extent, cuts, -0.22, 0.18) if cuts else 1.0
    drawn = jax.random.normal(stream_key, extent, jnp.float32) * spread * gain
    return jnp.minimum(jnp.maximum(drawn, -reach), reach).astype(held_as)


def setup_inputs(seed: int = 0) -> dict:
    keys = jax.random.split(jax.random.key(seed), 9)
    return {
        "query": draw_query(jax.random.fold_in(keys[8], 71), 0),
        "out_grad": normal_values(keys[1], (QC, L, D), 1.0, 6.0, ((0, 2), (1, 16))),
        "forward_out": normal_values(keys[2], (QC, L, D), 1.0, 6.0, ((0, 2), (1, 16))),
        "key_codes": draw_key_codes(jax.random.fold_in(keys[8], 71), 0),
        "key_scale": draw_key_scale(jax.random.fold_in(keys[8], 71), 0),
        "value_codes": draw_value_codes(jax.random.fold_in(keys[8], 71), 0),
        "value_scale": draw_value_scale(jax.random.fold_in(keys[8], 71), 0),
        "pairing": draw_pairing(jax.random.fold_in(keys[8], 71), 0),
    }


def dequantize(codes, scales):
    count, length, width = codes.shape
    head_count = scales.shape[2]
    values = codes.astype(jnp.float32).reshape(count, length, head_count, width // head_count) * scales.astype(jnp.float32)[..., None]
    return values.reshape(count, length, width).astype(jnp.bfloat16)


def per_head(array):
    return array.reshape(array.shape[0], L, H, HD).transpose(2, 0, 1, 3)


def to_rows(array):
    return array.transpose(1, 2, 0, 3).reshape(array.shape[1], L, D)


def reference(query, out_grad, forward_out, key_codes, key_scale, value_codes, value_scale, pairing):
    softmax_scale = HD ** -0.5
    key_full = dequantize(key_codes, key_scale)
    value_full = dequantize(value_codes, value_scale)
    product = out_grad.astype(jnp.float32) * forward_out.astype(jnp.float32)
    row_dots = jnp.sum(product.reshape(QC, L, H, HD), axis=-1).transpose(2, 0, 1)

    def one_head(inputs):
        query_head, grad_head, dot_head, key_head, value_head = inputs
        key_acc = jnp.zeros((KC, L, HD), jnp.float32)
        value_acc = jnp.zeros((KC, L, HD), jnp.float32)
        query_out = []
        for block_pos in range(QC):
            chosen = pairing[block_pos]
            key_set = jnp.take(key_head, chosen, axis=0).reshape(2 * L, HD)
            value_set = jnp.take(value_head, chosen, axis=0).reshape(2 * L, HD)
            scores = jnp.dot(query_head[block_pos], key_set.T, preferred_element_type=jnp.float32) * softmax_scale
            highest = jnp.max(scores, axis=1)
            weights = jnp.exp(scores - highest[:, None])
            probs = weights / jnp.sum(weights, axis=1)[:, None]
            rounded = probs.astype(jnp.bfloat16)
            value_grad = jnp.dot(rounded.T, grad_head[block_pos], preferred_element_type=jnp.float32)
            prob_grad = jnp.dot(grad_head[block_pos], value_set.T, preferred_element_type=jnp.float32)
            score_grad = (probs * (prob_grad - dot_head[block_pos][:, None]) * softmax_scale).astype(jnp.bfloat16)
            query_out.append(jnp.dot(score_grad, key_set, preferred_element_type=jnp.float32).astype(jnp.bfloat16))
            key_grad = jnp.dot(score_grad.T, query_head[block_pos], preferred_element_type=jnp.float32)
            key_acc = key_acc.at[chosen].add(key_grad.reshape(2, L, HD))
            value_acc = value_acc.at[chosen].add(value_grad.reshape(2, L, HD))
        return jnp.stack(query_out), key_acc.astype(jnp.bfloat16), value_acc.astype(jnp.bfloat16)

    grad_q, grad_k, grad_v = lax.map(one_head, (per_head(query), per_head(out_grad), row_dots, per_head(key_full), per_head(value_full)))
    return to_rows(grad_q), to_rows(grad_k), to_rows(grad_v)
```

```python
import functools
import math

import jax
import jax.numpy as jnp
from jax import lax
from jax.experimental import pallas as pl
from jax.experimental.pallas import tpu as pltpu
from jax.sharding import Mesh, PartitionSpec as P

HD = 128
SCALE = HD ** -0.5
ROWS = 256
NT = (((1,), (1,)), ((), ()))
NN = (((1,), (0,)), ((), ()))


def dot(a, b, dims):
    return lax.dot_general(a, b, dims, preferred_element_type=jnp.float32)


def grads_kernel(
    core_ref, bias_ref, q_own, g_own, o_own, swapped, k_ref, v_ref,
    dq_own, dq_in, dk_ref, dv_ref, q_all, g_all, dots, dq_all, dk_acc, dv_acc,
):
    own = q_own.shape[0]
    rows = 2 * own
    keys = k_ref.shape[0]
    q_all[:own] = q_own[...]
    q_all[own:] = swapped[0]
    g_all[:own] = g_own[...]
    g_all[own:] = swapped[1]
    ones = jnp.ones((8, HD), jnp.bfloat16)
    for part, (grad, out) in enumerate(((g_own[...], o_own[...]), (swapped[1], swapped[2]))):
        product = grad.astype(jnp.float32) * out.astype(jnp.float32)
        high = product.astype(jnp.bfloat16)
        low = (product - high.astype(jnp.float32)).astype(jnp.bfloat16)
        dots[:, part * own:(part + 1) * own] = dot(ones, high, NT) + dot(ones, low, NT)
    k_all = k_ref[...]
    v_all = v_ref[...]
    k_turned = k_all.astype(jnp.float32).T.astype(jnp.bfloat16)
    dk_acc[...] = jnp.zeros_like(dk_acc)
    dv_acc[...] = jnp.zeros_like(dv_acc)
    for start in range(0, rows, ROWS):
        size = min(ROWS, rows - start)
        at = pl.ds(start, size)
        q = q_all[at, :]
        g = g_all[at, :]
        bias = bias_ref[:, :, :, :, at]
        scores = dot(k_all, q, NT)
        span = keys // (bias.shape[0] * bias.shape[1] * bias.shape[2])
        masked = scores.reshape(bias.shape[:3] + (span, size)) + bias
        masked = masked.reshape(keys, size)
        highest = jnp.max(masked, axis=0, keepdims=True)
        weights = jnp.exp2((masked - highest) * (SCALE * math.log2(math.e)))
        probs = weights * (1.0 / jnp.sum(weights, axis=0, keepdims=True))
        dv_acc[...] += dot(probs.astype(jnp.bfloat16), g, NN)
        prob_grad = dot(v_all, g, NT)
        score_grad = (probs * (prob_grad - dots[0:1, at]) * SCALE).astype(jnp.bfloat16)
        dk_acc[...] += dot(score_grad, q, NN)
        dq_all[at, :] = dot(k_turned, score_grad, NN).T.astype(jnp.bfloat16)
    dq_own[...] = dq_all[:own]
    dq_in[...] = dq_all[own:]
    dk_ref[...] = dk_acc[...].astype(jnp.bfloat16)
    dv_ref[...] = dv_acc[...].astype(jnp.bfloat16)


def local_grads(core, bias, q, g, o, swapped, keys, values):
    own, half = q.shape[0], q.shape[1] // 2
    heads = half // HD
    count = keys.shape[0]
    offset = (core * heads).reshape(1).astype(jnp.int32)
    mine = pl.BlockSpec((own, HD), lambda h, c: (0, c[0] + h))
    column = pl.BlockSpec((own, HD), lambda h, c: (0, h))
    table = pl.BlockSpec((count, HD), lambda h, c: (0, h))
    return pl.pallas_call(
        grads_kernel,
        grid_spec=pltpu.PrefetchScalarGridSpec(
            num_scalar_prefetch=1,
            grid=(heads,),
            in_specs=[
                pl.BlockSpec(bias.shape, lambda h, c: (0, 0, 0, 0, 0)),
                mine, mine, mine,
                pl.BlockSpec((3, own, HD), lambda h, c: (0, 0, h)),
                table, table,
            ],
            out_specs=[column, column, table, table],
            scratch_shapes=[
                pltpu.VMEM((2 * own, HD), jnp.bfloat16),
                pltpu.VMEM((2 * own, HD), jnp.bfloat16),
                pltpu.VMEM((8, 2 * own), jnp.float32),
                pltpu.VMEM((2 * own, HD), jnp.bfloat16),
                pltpu.VMEM((count, HD), jnp.float32),
                pltpu.VMEM((count, HD), jnp.float32),
            ],
        ),
        out_shape=[
            jax.ShapeDtypeStruct((own, half), jnp.bfloat16),
            jax.ShapeDtypeStruct((own, half), jnp.bfloat16),
            jax.ShapeDtypeStruct((count, half), jnp.bfloat16),
            jax.ShapeDtypeStruct((count, half), jnp.bfloat16),
        ],
        compiler_params=pltpu.CompilerParams(vmem_limit_bytes=40 * 2 ** 20),
        cost_estimate=pl.CostEstimate(
            flops=20 * own * count * half, bytes_accessed=14 * own * half + 8 * count * half,
            transcendentals=2 * own * count * heads,
        ),
    )(offset, bias, q, g, o, swapped, keys, values)


def dequantize(codes, scales):
    count, length, width = codes.shape
    heads = scales.shape[2]
    values = (
        codes.astype(jnp.float32).reshape(count, length, heads, width // heads)
        * scales.astype(jnp.float32)[..., None]
    )
    return values.reshape(count, length, width).astype(jnp.bfloat16)


def swap(array):
    return lax.ppermute(array, "core", [(0, 1), (1, 0)])


def in_order(core, mine, other, axis):
    return jnp.where(
        core == 0,
        jnp.concatenate([mine, other], axis=axis),
        jnp.concatenate([other, mine], axis=axis),
    )


def on_device(group_count, query, out_grad, forward_out, key_codes, key_scale, value_codes, value_scale, pairing):
    core = lax.axis_index("core")
    group = lax.axis_index("grp")
    blocks, tokens, width = query.shape
    half = width // 2
    own = blocks * tokens
    table = jnp.stack([dequantize(key_codes, key_scale), dequantize(value_codes, value_scale)])
    kept = lax.dynamic_slice_in_dim(table, core * half, half, axis=3)
    other = swap(lax.dynamic_slice_in_dim(table, (1 - core) * half, half, axis=3))
    shard = in_order(core, kept, other, 2)
    kv_local, kv_tokens = shard.shape[1:3]
    gathered = [
        lax.all_gather(shard[i].reshape(kv_local * kv_tokens, half), ("grp", "chip"), axis=0, tiled=True)
        for i in range(2)
    ]
    flat = [a.reshape(own, width) for a in (query, out_grad, forward_out)]
    swapped = swap(jnp.stack([
        lax.dynamic_slice_in_dim(a, (1 - core) * half, half, axis=1) for a in flat
    ]))
    chips = gathered[0].shape[0] // (group_count * kv_local * kv_tokens)
    chosen = lax.dynamic_slice_in_dim(pairing, group * blocks, blocks, axis=0)
    hit = jnp.any(chosen[None] == jnp.arange(group_count * kv_local)[:, None, None], axis=2)
    bias = jnp.where(hit, 0.0, -jnp.inf).astype(jnp.float32)
    bias = jnp.tile(jnp.repeat(bias, tokens, axis=1), (1, 2))
    bias = bias.reshape(group_count, 1, kv_local, 1, 2 * own)
    bias = jnp.broadcast_to(bias, (group_count, chips, kv_local, 1, 2 * own))
    dq_mine, dq_other, dk, dv = local_grads(core, bias, *flat, swapped, *gathered)
    dq = in_order(core, dq_mine, swap(dq_other), 1).reshape(query.shape)
    sums = [
        lax.psum_scatter(a, ("grp", "chip"), scatter_dimension=0, tiled=True)
        .reshape(kv_local, kv_tokens, half)
        for a in (dk, dv)
    ]
    length = kv_tokens // 2
    sums = jnp.stack(sums)
    kept = lax.dynamic_slice_in_dim(sums, core * length, length, axis=2)
    other = swap(lax.dynamic_slice_in_dim(sums, (1 - core) * length, length, axis=2))
    grads = in_order(core, kept, other, 3)
    return dq, grads[0], grads[1]


def solution(mesh):
    groups, heads = mesh.shape["grp"], mesh.shape["head"]
    split = Mesh(mesh.devices.reshape(groups, heads // 2, 2), ("grp", "chip", "core"))
    spec = P("grp", ("chip", "core"), None)
    return jax.shard_map(
        functools.partial(on_device, groups),
        mesh=split,
        in_specs=(spec,) * 7 + (P(),),
        out_specs=(spec,) * 3,
        check_vma=False,
    )
```

```python
import functools
import math

import jax
import jax.numpy as jnp
from jax import lax
from jax.experimental import pallas as pl
from jax.experimental.pallas import tpu as pltpu
from jax.sharding import Mesh, PartitionSpec as P

HD = 128
SCALE = HD ** -0.5
ROWS = 256
NT = (((1,), (1,)), ((), ()))
NN = (((1,), (0,)), ((), ()))


def dot(a, b, dims):
    return lax.dot_general(a, b, dims, preferred_element_type=jnp.float32)


def grads_kernel(
    core_ref, bias_ref, q_own, g_own, o_own, swapped, k_ref, v_ref,
    dq_own, dq_in, dk_ref, dv_ref, q_all, g_all, dots, dq_all, dk_acc, dv_acc,
):
    own = q_own.shape[0]
    rows = 2 * own
    keys = k_ref.shape[0]
    q_all[:own] = q_own[...]
    q_all[own:] = swapped[0]
    g_all[:own] = g_own[...]
    g_all[own:] = swapped[1]
    ones = jnp.ones((8, HD), jnp.bfloat16)
    for part, (grad, out) in enumerate(((g_own[...], o_own[...]), (swapped[1], swapped[2]))):
        product = grad.astype(jnp.float32) * out.astype(jnp.float32)
        high = product.astype(jnp.bfloat16)
        low = (product - high.astype(jnp.float32)).astype(jnp.bfloat16)
        dots[:, part * own:(part + 1) * own] = dot(ones, high, NT) + dot(ones, low, NT)
    k_all = k_ref[...]
    v_all = v_ref[...]
    k_turned = k_all.astype(jnp.float32).T.astype(jnp.bfloat16)
    dk_acc[...] = jnp.zeros_like(dk_acc)
    dv_acc[...] = jnp.zeros_like(dv_acc)
    for start in range(0, rows, ROWS):
        size = min(ROWS, rows - start)
        at = pl.ds(start, size)
        q = q_all[at, :]
        g = g_all[at, :]
        bias = bias_ref[:, :, :, :, at]
        scores = dot(k_all, q, NT)
        span = keys // (bias.shape[0] * bias.shape[1] * bias.shape[2])
        masked = scores.reshape(bias.shape[:3] + (span, size)) + bias
        masked = masked.reshape(keys, size)
        highest = jnp.max(masked, axis=0, keepdims=True)
        weights = jnp.exp2((masked - highest) * (SCALE * math.log2(math.e)))
        probs = weights * (1.0 / jnp.sum(weights, axis=0, keepdims=True))
        dv_acc[...] += dot(probs.astype(jnp.bfloat16), g, NN)
        prob_grad = dot(v_all, g, NT)
        score_grad = (probs * (prob_grad - dots[0:1, at]) * SCALE).astype(jnp.bfloat16)
        dk_acc[...] += dot(score_grad, q, NN)
        dq_all[at, :] = dot(k_turned, score_grad, NN).T.astype(jnp.bfloat16)
    dq_own[...] = dq_all[:own]
    dq_in[...] = dq_all[own:]
    dk_ref[...] = dk_acc[...].astype(jnp.bfloat16)
    dv_ref[...] = dv_acc[...].astype(jnp.bfloat16)


def local_grads(core, bias, q, g, o, swapped, keys, values):
    own, half = q.shape[0], q.shape[1] // 2
    heads = half // HD
    count = keys.shape[0]
    offset = (core * heads).reshape(1).astype(jnp.int32)
    mine = pl.BlockSpec((own, HD), lambda h, c: (0, c[0] + h))
    column = pl.BlockSpec((own, HD), lambda h, c: (0, h))
    table = pl.BlockSpec((count, HD), lambda h, c: (0, h))
    return pl.pallas_call(
        grads_kernel,
        grid_spec=pltpu.PrefetchScalarGridSpec(
            num_scalar_prefetch=1,
            grid=(heads,),
            in_specs=[
                pl.BlockSpec(bias.shape, lambda h, c: (0, 0, 0, 0, 0)),
                mine, mine, mine,
                pl.BlockSpec((3, own, HD), lambda h, c: (0, 0, h)),
                table, table,
            ],
            out_specs=[column, column, table, table],
            scratch_shapes=[
                pltpu.VMEM((2 * own, HD), jnp.bfloat16),
                pltpu.VMEM((2 * own, HD), jnp.bfloat16),
                pltpu.VMEM((8, 2 * own), jnp.float32),
                pltpu.VMEM((2 * own, HD), jnp.bfloat16),
                pltpu.VMEM((count, HD), jnp.float32),
                pltpu.VMEM((count, HD), jnp.float32),
            ],
        ),
        out_shape=[
            jax.ShapeDtypeStruct((own, half), jnp.bfloat16),
            jax.ShapeDtypeStruct((own, half), jnp.bfloat16),
            jax.ShapeDtypeStruct((count, half), jnp.bfloat16),
            jax.ShapeDtypeStruct((count, half), jnp.bfloat16),
        ],
        compiler_params=pltpu.CompilerParams(vmem_limit_bytes=40 * 2 ** 20),
        cost_estimate=pl.CostEstimate(
            flops=20 * own * count * half, bytes_accessed=14 * own * half + 8 * count * half,
            transcendentals=2 * own * count * heads,
        ),
    )(offset, bias, q, g, o, swapped, keys, values)


MESH = pl.DeviceIdType.MESH


def place():
    group, chip, core = (lax.axis_index(name) for name in ("grp", "chip", "core"))
    line, pair = chip // 2, chip % 2
    beside = ((1 - group, chip, core), (group, line * 2 + 1 - pair, core))
    return group, line, pair, beside, lambda at: (group, at * 2 + pair, core)


def meet(lines, line, beside, along):
    barrier = pltpu.get_barrier_semaphore()
    for device in beside:
        pl.semaphore_signal(barrier, inc=1, device_id=device, device_id_type=MESH)
    for side in (-1, 1):
        @pl.when((line + side >= 0) & (line + side < lines))
        def _():
            pl.semaphore_signal(barrier, inc=1, device_id=along(line + side), device_id_type=MESH)
    count = 2 + (line > 0).astype(jnp.int32) + (line < lines - 1).astype(jnp.int32)
    pl.semaphore_wait(barrier, count)


def remote(src, dst, send, recv, device):
    return pltpu.make_async_remote_copy(
        src_ref=src, dst_ref=dst, send_sem=send, recv_sem=recv, device_id=device, device_id_type=MESH
    )


def each(lines, line, distance, body):
    for side in ((-1, 1) if distance else (0,)):
        at = line + side * distance
        if distance:
            @pl.when((at >= 0) & (at < lines))
            def _():
                body(side, at)
        else:
            body(side, at)


def gather_kernel(
    lines, k_in, v_in, k_out, v_out,
    local_sem, z_send, z_recv, s_send, s_recv, f_send, f_recv,
):
    group, line, pair, beside, along = place()
    ins, outs = (k_in, v_in), (k_out, v_out)
    locals_ = [
        pltpu.make_async_copy(ins[kind], outs[kind].at[group, line, pair], local_sem.at[kind])
        for kind in range(2)
    ]
    for copy in locals_:
        copy.start()
    meet(lines, line, beside, along)

    def relay(kind, side, at, first):
        slot = outs[kind].at[group, at, pair]
        way = (side + 1) // 2
        return remote(
            ins[kind] if first else slot, slot, z_send.at[kind, way, at], z_recv.at[kind, at],
            along(line + side),
        )

    def sideways(kind, way, at, first):
        slot = outs[kind].at[group, at, pair]
        return remote(
            ins[kind] if first else slot, slot, s_send.at[kind, way, at], s_recv.at[kind, way, at],
            beside[way],
        )

    def forward(kind, at):
        slot = outs[0].at[1 - group, at, pair] if kind == 0 else outs[1].at[group, at, 1 - pair]
        return remote(slot, slot, f_send.at[kind, at], f_recv.at[kind, at], beside[1 - kind])

    def spread(distance):
        def body(side, at):
            for kind in range(2):
                if distance:
                    relay(kind, side, at, False).wait_recv()
                for onward in ((-1, 1) if distance == 0 else (-side,)):
                    @pl.when((line + onward >= 0) & (line + onward < lines))
                    def _():
                        relay(kind, onward, at, distance == 0).start()
                for way in (kind, 1 - kind):
                    sideways(kind, way, at, distance == 0).start()
        each(lines, line, distance, body)

    def across(distance):
        def body(side, at):
            for kind in range(2):
                sideways(kind, kind, at, False).wait_recv()
                forward(kind, at).start()
        each(lines, line, distance, body)

    def finish(distance):
        def body(side, at):
            for kind in range(2):
                sideways(kind, 1 - kind, at, False).wait_recv()
                forward(kind, at).wait_recv()
                forward(kind, at).wait_send()
                for way in range(2):
                    sideways(kind, way, at, False).wait_send()
                for onward in ((-1, 1) if distance == 0 else (-side,)):
                    @pl.when((line + onward >= 0) & (line + onward < lines))
                    def _():
                        relay(kind, onward, at, False).wait_send()
        each(lines, line, distance, body)

    spread(0)
    for distance in range(1, lines):
        spread(distance)
        across(distance - 1)
    across(lines - 1)
    for distance in range(lines):
        finish(distance)
    for copy in locals_:
        copy.wait()


def gather(keys, values, lines):
    shape = jax.ShapeDtypeStruct((2, lines, 2) + keys.shape, keys.dtype)
    anywhere = pl.BlockSpec(memory_space=pl.ANY)
    dma = pltpu.SemaphoreType.DMA
    return pl.pallas_call(
        functools.partial(gather_kernel, lines),
        in_specs=[anywhere] * 2,
        out_specs=[anywhere] * 2,
        out_shape=[shape] * 2,
        scratch_shapes=[
            dma((2,)), dma((2, 2, lines)), dma((2, lines)), dma((2, 2, lines)), dma((2, 2, lines)),
            dma((2, lines)), dma((2, lines)),
        ],
        compiler_params=pltpu.CompilerParams(collective_id=0, has_side_effects=True),
    )(keys, values)


def scatter_kernel(
    lines, k_ref, v_ref, out_ref, first_in, second_out, second_in, line_out, line_in, total,
    a_send, a_recv, b_send, b_recv, z_send, z_recv,
):
    group, line, pair, beside, along = place()
    refs = (k_ref, v_ref)
    meet(lines, line, beside, along)

    def first(kind, at):
        src = k_ref.at[1 - group, at] if kind == 0 else v_ref.at[:, at, 1 - pair]
        return remote(src, first_in.at[kind, at], a_send.at[kind, at], a_recv.at[kind, at], beside[kind])

    def second(kind, at):
        return remote(
            second_out.at[kind, at], second_in.at[kind, at], b_send.at[kind, at], b_recv.at[kind, at],
            beside[1 - kind],
        )

    def pass_on(kind, side, at):
        way = (side + 1) // 2
        return remote(
            line_out.at[kind, at], line_in.at[kind, way, at], z_send.at[kind, at],
            z_recv.at[kind, way, at], along(line + side),
        )

    def start(distance):
        def body(side, at):
            for kind in range(2):
                first(kind, at).start()
        each(lines, line, distance, body)

    def halve(distance):
        def body(side, at):
            for kind in range(2):
                first(kind, at).wait_recv()
                if kind == 0:
                    mine, come = k_ref[group, at, 1 - pair], first_in[0, at, 1 - pair]
                else:
                    mine, come = v_ref[1 - group, at, pair], first_in[1, at, 1 - group]
                second_out[kind, at] = (mine.astype(jnp.float32) + come.astype(jnp.float32)).astype(jnp.bfloat16)
                second(kind, at).start()
        each(lines, line, distance, body)

    def collect(distance):
        def body(side, at):
            for kind in range(2):
                second(kind, at).wait_recv()
                come = first_in[kind, at, pair if kind == 0 else group]
                total[kind] = (
                    refs[kind][group, at, pair].astype(jnp.float32) + come.astype(jnp.float32)
                    + second_in[kind, at].astype(jnp.float32)
                )
                for way in ((-1, 1) if distance == 0 else (side,)):
                    @pl.when((line - way >= 0) & (line - way < lines))
                    def _():
                        pass_on(kind, way, at).wait_recv()
                        total[kind] += line_in[kind, (way + 1) // 2, at].astype(jnp.float32)
                if distance:
                    line_out[kind, at] = total[kind].astype(jnp.bfloat16)
                    pass_on(kind, side, at).start()
                else:
                    out_ref[kind] = total[kind].astype(jnp.bfloat16)
        each(lines, line, distance, body)

    def finish(distance):
        def body(side, at):
            for kind in range(2):
                first(kind, at).wait_send()
                second(kind, at).wait_send()
                if distance:
                    pass_on(kind, side, at).wait_send()
        each(lines, line, distance, body)

    order = list(range(lines - 1, -1, -1))
    for turn in range(lines + 3):
        if turn < lines:
            start(order[turn])
        if 0 <= turn - 2 < lines:
            halve(order[turn - 2])
        if 0 <= turn - 3 < lines:
            collect(order[turn - 3])
    for distance in range(lines):
        finish(distance)


def scatter(dk, dv):
    lines, rows, half = dk.shape[1], dk.shape[3], dk.shape[4]
    here = pl.BlockSpec(memory_space=pltpu.VMEM)
    dma = pltpu.SemaphoreType.DMA
    return pl.pallas_call(
        functools.partial(scatter_kernel, lines),
        in_specs=[here] * 2,
        out_specs=here,
        out_shape=jax.ShapeDtypeStruct((2, rows, half), jnp.bfloat16),
        scratch_shapes=[
            pltpu.VMEM((2, lines, 2, rows, half), jnp.bfloat16),
            pltpu.VMEM((2, lines, rows, half), jnp.bfloat16),
            pltpu.VMEM((2, lines, rows, half), jnp.bfloat16),
            pltpu.VMEM((2, lines, rows, half), jnp.bfloat16),
            pltpu.VMEM((2, 2, lines, rows, half), jnp.bfloat16),
            pltpu.VMEM((2, rows, half), jnp.float32),
            dma((2, lines)), dma((2, lines)), dma((2, lines)), dma((2, lines)),
            dma((2, lines)), dma((2, 2, lines)),
        ],
        compiler_params=pltpu.CompilerParams(
            collective_id=1, has_side_effects=True, vmem_limit_bytes=56 * 2 ** 20,
        ),
    )(dk, dv)


def dequantize(codes, scales):
    count, length, width = codes.shape
    heads = scales.shape[2]
    values = (
        codes.astype(jnp.float32).reshape(count, length, heads, width // heads)
        * scales.astype(jnp.float32)[..., None]
    )
    return values.reshape(count, length, width).astype(jnp.bfloat16)


def swap(array):
    return lax.ppermute(array, "core", [(0, 1), (1, 0)])


def in_order(core, mine, other, axis):
    return jnp.where(
        core == 0,
        jnp.concatenate([mine, other], axis=axis),
        jnp.concatenate([other, mine], axis=axis),
    )


def on_device(group_count, lines, query, out_grad, forward_out, key_codes, key_scale, value_codes, value_scale, pairing):
    core = lax.axis_index("core")
    group = lax.axis_index("grp")
    blocks, tokens, width = query.shape
    half = width // 2
    own = blocks * tokens
    table = jnp.stack([dequantize(key_codes, key_scale), dequantize(value_codes, value_scale)])
    kept = lax.dynamic_slice_in_dim(table, core * half, half, axis=3)
    other = swap(lax.dynamic_slice_in_dim(table, (1 - core) * half, half, axis=3))
    shard = in_order(core, kept, other, 2)
    kv_local, kv_tokens = shard.shape[1:3]
    shard = shard.reshape(2, kv_local * kv_tokens, half)
    gathered = [a.reshape(-1, half) for a in gather(shard[0], shard[1], lines)]
    flat = [a.reshape(own, width) for a in (query, out_grad, forward_out)]
    swapped = swap(jnp.stack([
        lax.dynamic_slice_in_dim(a, (1 - core) * half, half, axis=1) for a in flat
    ]))
    chips = gathered[0].shape[0] // (group_count * kv_local * kv_tokens)
    chosen = lax.dynamic_slice_in_dim(pairing, group * blocks, blocks, axis=0)
    hit = jnp.any(chosen[None] == jnp.arange(group_count * kv_local)[:, None, None], axis=2)
    bias = jnp.where(hit, 0.0, -jnp.inf).astype(jnp.float32)
    bias = jnp.tile(jnp.repeat(bias, tokens, axis=1), (1, 2))
    bias = bias.reshape(group_count, 1, kv_local, 1, 2 * own)
    bias = jnp.broadcast_to(bias, (group_count, chips, kv_local, 1, 2 * own))
    dq_mine, dq_other, dk, dv = local_grads(core, bias, *flat, swapped, *gathered)
    dq = in_order(core, dq_mine, swap(dq_other), 1).reshape(query.shape)
    split = (2, lines, 2, kv_local * kv_tokens, half)
    sums = scatter(dk.reshape(split), dv.reshape(split)).reshape(2, kv_local, kv_tokens, half)
    length = kv_tokens // 2
    kept = lax.dynamic_slice_in_dim(sums, core * length, length, axis=2)
    other = swap(lax.dynamic_slice_in_dim(sums, (1 - core) * length, length, axis=2))
    grads = in_order(core, kept, other, 3)
    return dq, grads[0], grads[1]


def solution(mesh):
    groups, heads = mesh.shape["grp"], mesh.shape["head"]
    split = Mesh(mesh.devices.reshape(groups, heads // 2, 2), ("grp", "chip", "core"))
    spec = P("grp", ("chip", "core"), None)
    return jax.shard_map(
        functools.partial(on_device, groups, heads // 4),
        mesh=split,
        in_specs=(spec,) * 7 + (P(),),
        out_specs=(spec,) * 3,
        check_vma=False,
    )
```

```python
import functools
import math

import jax
import jax.numpy as jnp
from jax import lax
from jax.experimental import pallas as pl
from jax.experimental.pallas import tpu as pltpu
from jax.sharding import Mesh, PartitionSpec as P

HD = 128
SCALE = HD ** -0.5
ROWS = 256
NT = (((1,), (1,)), ((), ()))
NN = (((1,), (0,)), ((), ()))


def dot(a, b, dims):
    return lax.dot_general(a, b, dims, preferred_element_type=jnp.float32)


MESH = pl.DeviceIdType.MESH


def place():
    group, chip, core = (lax.axis_index(name) for name in ("grp", "chip", "core"))
    line, pair = chip // 2, chip % 2
    beside = ((1 - group, chip, core), (group, line * 2 + 1 - pair, core))
    return group, line, pair, beside, lambda at: (group, at * 2 + pair, core)


def meet(lines, line, beside, along):
    barrier = pltpu.get_barrier_semaphore()
    for device in beside:
        pl.semaphore_signal(barrier, inc=1, device_id=device, device_id_type=MESH)
    for side in (-1, 1):
        @pl.when((line + side >= 0) & (line + side < lines))
        def _():
            pl.semaphore_signal(barrier, inc=1, device_id=along(line + side), device_id_type=MESH)
    count = 2 + (line > 0).astype(jnp.int32) + (line < lines - 1).astype(jnp.int32)
    pl.semaphore_wait(barrier, count)


def remote(src, dst, send, recv, device):
    return pltpu.make_async_remote_copy(
        src_ref=src, dst_ref=dst, send_sem=send, recv_sem=recv, device_id=device, device_id_type=MESH
    )


def each(lines, line, distance, body):
    for side in ((-1, 1) if distance else (0,)):
        at = line + side * distance
        if distance:
            @pl.when((at >= 0) & (at < lines))
            def _():
                body(side, at)
        else:
            body(side, at)


def gather_steps(
    lines, k_in, v_in, k_out, v_out,
    local_sem, z_send, z_recv, s_send, s_recv, f_send, f_recv,
):
    group, line, pair, beside, along = place()
    ins, outs = (k_in, v_in), (k_out, v_out)
    locals_ = [
        pltpu.make_async_copy(ins[kind], outs[kind].at[group, line, pair], local_sem.at[kind])
        for kind in range(2)
    ]

    def begin():
        for copy in locals_:
            copy.start()
        meet(lines, line, beside, along)

    def relay(kind, side, at, first):
        slot = outs[kind].at[group, at, pair]
        way = (side + 1) // 2
        return remote(
            ins[kind] if first else slot, slot, z_send.at[kind, way, at], z_recv.at[kind, at],
            along(line + side),
        )

    def sideways(kind, way, at, first):
        slot = outs[kind].at[group, at, pair]
        return remote(
            ins[kind] if first else slot, slot, s_send.at[kind, way, at], s_recv.at[kind, way, at],
            beside[way],
        )

    def forward(kind, at):
        slot = outs[0].at[1 - group, at, pair] if kind == 0 else outs[1].at[group, at, 1 - pair]
        return remote(slot, slot, f_send.at[kind, at], f_recv.at[kind, at], beside[1 - kind])

    def spread(distance):
        def body(side, at):
            for kind in range(2):
                if distance:
                    relay(kind, side, at, False).wait_recv()
                for onward in ((-1, 1) if distance == 0 else (-side,)):
                    @pl.when((line + onward >= 0) & (line + onward < lines))
                    def _():
                        relay(kind, onward, at, distance == 0).start()
                for way in (kind, 1 - kind):
                    sideways(kind, way, at, distance == 0).start()
        each(lines, line, distance, body)

    def across(distance):
        def body(side, at):
            for kind in range(2):
                sideways(kind, kind, at, False).wait_recv()
                forward(kind, at).start()
        each(lines, line, distance, body)

    def finish(distance):
        def body(side, at):
            for kind in range(2):
                sideways(kind, 1 - kind, at, False).wait_recv()
                forward(kind, at).wait_recv()
                forward(kind, at).wait_send()
                for way in range(2):
                    sideways(kind, way, at, False).wait_send()
                for onward in ((-1, 1) if distance == 0 else (-side,)):
                    @pl.when((line + onward >= 0) & (line + onward < lines))
                    def _():
                        relay(kind, onward, at, False).wait_send()
        each(lines, line, distance, body)

    def end():
        for distance in range(lines):
            finish(distance)
        for copy in locals_:
            copy.wait()

    def turn(distance):
        if distance == 0:
            begin()
        if distance < lines:
            spread(distance)
        if distance:
            across(distance - 1)

    turns = [functools.partial(turn, distance) for distance in range(lines + 1)]
    return turns, end


def run(steps):
    turns, end = steps
    for turn in turns:
        turn()
    end()


def gather_kernel(lines, *refs):
    run(gather_steps(lines, *refs))


def gather_scratch(lines):
    dma = pltpu.SemaphoreType.DMA
    return [
        dma((2,)), dma((2, 2, lines)), dma((2, lines)), dma((2, 2, lines)), dma((2, 2, lines)),
        dma((2, lines)), dma((2, lines)),
    ]


def gather(keys, values, lines):
    shape = jax.ShapeDtypeStruct((2, lines, 2) + keys.shape, keys.dtype)
    anywhere = pl.BlockSpec(memory_space=pl.ANY)
    return pl.pallas_call(
        functools.partial(gather_kernel, lines),
        in_specs=[anywhere] * 2,
        out_specs=[anywhere] * 2,
        out_shape=[shape] * 2,
        scratch_shapes=gather_scratch(lines),
        compiler_params=pltpu.CompilerParams(collective_id=0, has_side_effects=True),
        cost_estimate=pl.CostEstimate(flops=0, bytes_accessed=2 ** 26, transcendentals=0),
    )(keys, values)


def scatter_steps(
    lines, k_ref, v_ref, out_ref, first_in, second_out, second_in, line_out, line_in, total,
    a_send, a_recv, b_send, b_recv, z_send, z_recv,
):
    group, line, pair, beside, along = place()
    refs = (k_ref, v_ref)

    def first(kind, at):
        src = k_ref.at[1 - group, at] if kind == 0 else v_ref.at[:, at, 1 - pair]
        return remote(src, first_in.at[kind, at], a_send.at[kind, at], a_recv.at[kind, at], beside[kind])

    def second(kind, at):
        return remote(
            second_out.at[kind, at], second_in.at[kind, at], b_send.at[kind, at], b_recv.at[kind, at],
            beside[1 - kind],
        )

    def pass_on(kind, side, at):
        way = (side + 1) // 2
        return remote(
            line_out.at[kind, at], line_in.at[kind, way, at], z_send.at[kind, at],
            z_recv.at[kind, way, at], along(line + side),
        )

    def start(distance):
        def body(side, at):
            for kind in range(2):
                first(kind, at).start()
        each(lines, line, distance, body)

    def halve(distance):
        def body(side, at):
            for kind in range(2):
                first(kind, at).wait_recv()
                if kind == 0:
                    mine, come = k_ref[group, at, 1 - pair], first_in[0, at, 1 - pair]
                else:
                    mine, come = v_ref[1 - group, at, pair], first_in[1, at, 1 - group]
                second_out[kind, at] = (mine.astype(jnp.float32) + come.astype(jnp.float32)).astype(jnp.bfloat16)
                second(kind, at).start()
        each(lines, line, distance, body)

    def collect(distance):
        def body(side, at):
            for kind in range(2):
                second(kind, at).wait_recv()
                come = first_in[kind, at, pair if kind == 0 else group]
                total[kind] = (
                    refs[kind][group, at, pair].astype(jnp.float32) + come.astype(jnp.float32)
                    + second_in[kind, at].astype(jnp.float32)
                )
                for way in ((-1, 1) if distance == 0 else (side,)):
                    @pl.when((line - way >= 0) & (line - way < lines))
                    def _():
                        pass_on(kind, way, at).wait_recv()
                        total[kind] += line_in[kind, (way + 1) // 2, at].astype(jnp.float32)
                if distance:
                    line_out[kind, at] = total[kind].astype(jnp.bfloat16)
                    pass_on(kind, side, at).start()
                else:
                    out_ref[kind] = total[kind].astype(jnp.bfloat16)
        each(lines, line, distance, body)

    def finish(distance):
        def body(side, at):
            for kind in range(2):
                first(kind, at).wait_send()
                second(kind, at).wait_send()
                if distance:
                    pass_on(kind, side, at).wait_send()
        each(lines, line, distance, body)

    order = list(range(lines - 1, -1, -1))

    def turn(count):
        if count == 0:
            meet(lines, line, beside, along)
        if count < lines:
            start(order[count])
        if 0 <= count - 2 < lines:
            halve(order[count - 2])
        if 0 <= count - 3 < lines:
            collect(order[count - 3])

    def end():
        for distance in range(lines):
            finish(distance)

    return [functools.partial(turn, count) for count in range(lines + 3)], end


def scatter_kernel(lines, *refs):
    run(scatter_steps(lines, *refs))


def scatter_scratch(lines, rows, width):
    dma = pltpu.SemaphoreType.DMA
    return [
        pltpu.VMEM((2, lines, 2, rows, width), jnp.bfloat16),
        pltpu.VMEM((2, lines, rows, width), jnp.bfloat16),
        pltpu.VMEM((2, lines, rows, width), jnp.bfloat16),
        pltpu.VMEM((2, lines, rows, width), jnp.bfloat16),
        pltpu.VMEM((2, 2, lines, rows, width), jnp.bfloat16),
        pltpu.VMEM((2, rows, width), jnp.float32),
        dma((2, lines)), dma((2, lines)), dma((2, lines)), dma((2, lines)),
        dma((2, lines)), dma((2, 2, lines)),
    ]


def scatter(dk, dv):
    lines, rows, half = dk.shape[1], dk.shape[3], dk.shape[4]
    here = pl.BlockSpec(memory_space=pltpu.VMEM)
    return pl.pallas_call(
        functools.partial(scatter_kernel, lines),
        in_specs=[here] * 2,
        out_specs=here,
        out_shape=jax.ShapeDtypeStruct((2, rows, half), jnp.bfloat16),
        scratch_shapes=scatter_scratch(lines, rows, half),
        compiler_params=pltpu.CompilerParams(
            collective_id=3, has_side_effects=True, vmem_limit_bytes=56 * 2 ** 20,
        ),
        cost_estimate=pl.CostEstimate(flops=0, bytes_accessed=2 ** 26, transcendentals=0),
    )(dk, dv)


def grads_body(
    refs, outs, scratch, tick,
):
    bias_ref, q_own, g_own, o_own, swapped, k_ref, v_ref = refs
    dq_own, dq_in, dk_ref, dv_ref = outs
    q_all, g_all, dots, dq_all, dk_acc, dv_acc = scratch
    own = q_own.shape[0]
    rows = 2 * own
    keys = k_ref.shape[0]
    q_all[:own] = q_own[...]
    q_all[own:] = swapped[0]
    g_all[:own] = g_own[...]
    g_all[own:] = swapped[1]
    ones = jnp.ones((8, HD), jnp.bfloat16)
    for part, (grad, out) in enumerate(((g_own[...], o_own[...]), (swapped[1], swapped[2]))):
        product = grad.astype(jnp.float32) * out.astype(jnp.float32)
        high = product.astype(jnp.bfloat16)
        low = (product - high.astype(jnp.float32)).astype(jnp.bfloat16)
        dots[:, part * own:(part + 1) * own] = dot(ones, high, NT) + dot(ones, low, NT)
    k_all = k_ref[...]
    v_all = v_ref[...]
    k_turned = k_all.astype(jnp.float32).T.astype(jnp.bfloat16)
    dk_acc[...] = jnp.zeros_like(dk_acc)
    dv_acc[...] = jnp.zeros_like(dv_acc)
    for index, start in enumerate(range(0, rows, ROWS)):
        tick(index)
        size = min(ROWS, rows - start)
        at = pl.ds(start, size)
        q = q_all[at, :]
        g = g_all[at, :]
        bias = bias_ref[:, :, :, :, at]
        scores = dot(k_all, q, NT)
        span = keys // (bias.shape[0] * bias.shape[1] * bias.shape[2])
        masked = scores.reshape(bias.shape[:3] + (span, size)) + bias
        masked = masked.reshape(keys, size)
        highest = jnp.max(masked, axis=0, keepdims=True)
        weights = jnp.exp2((masked - highest) * (SCALE * math.log2(math.e)))
        probs = weights * (1.0 / jnp.sum(weights, axis=0, keepdims=True))
        dv_acc[...] += dot(probs.astype(jnp.bfloat16), g, NN)
        prob_grad = dot(v_all, g, NT)
        score_grad = (probs * (prob_grad - dots[0:1, at]) * SCALE).astype(jnp.bfloat16)
        dk_acc[...] += dot(score_grad, q, NN)
        dq_all[at, :] = dot(k_turned, score_grad, NN).T.astype(jnp.bfloat16)
    dq_own[...] = dq_all[:own]
    dq_in[...] = dq_all[own:]
    dk_ref[...] = dk_acc[...].astype(jnp.bfloat16)
    dv_ref[...] = dv_acc[...].astype(jnp.bfloat16)


def grads_kernel(lines, heads, steps, moved_out, *refs):
    ins, rest = refs[:7], refs[7:]
    moved, rest = rest[:2], rest[2:]
    outs, rest = rest[:4], rest[4:]
    arrived, rest = rest[:moved_out], rest[moved_out:]
    scratch, extra = rest[:6], rest[6:]
    turns, end = steps(lines, *moved, *arrived, *extra)
    per_head = pl.cdiv(2 * ins[1].shape[0], ROWS)
    slots = per_head * heads
    head = pl.program_id(0)

    def tick(index):
        for count, turn in enumerate(turns):
            slot = count * slots // len(turns)
            if slot % per_head == index:
                pl.when(head == slot // per_head)(turn)

    grads_body(ins, outs, scratch, tick)
    pl.when(head == heads - 1)(end)


def local_grads(part, parts, lines, bias, q, g, o, swapped, keys, values, moved, gathering):
    own, half = q.shape[0], q.shape[1] // 2
    heads = half // HD // parts
    count, width = keys.shape[0], heads * HD
    first = part * heads
    mine = pl.BlockSpec((own, HD), lambda h: (0, lax.axis_index("core") * (heads * parts) + first + h))
    column = pl.BlockSpec((own, HD), lambda h: (0, h))
    table = pl.BlockSpec((count, HD), lambda h: (0, h))
    anywhere = pl.BlockSpec(memory_space=pl.ANY)
    here = pl.BlockSpec(memory_space=pltpu.VMEM)
    if gathering:
        steps, specs, extra_specs = gather_steps, [anywhere] * 2, [anywhere] * 2
        extra = [jax.ShapeDtypeStruct((2, lines, 2) + moved[0].shape, jnp.bfloat16)] * 2
        more = gather_scratch(lines)
    else:
        rows = moved[0].shape[3]
        steps, specs, extra_specs = scatter_steps, [here] * 2, [here]
        extra = [jax.ShapeDtypeStruct((2, rows, width), jnp.bfloat16)]
        more = scatter_scratch(lines, rows, width)
    return pl.pallas_call(
        functools.partial(grads_kernel, lines, heads, steps, len(extra)),
        grid=(heads,),
        in_specs=[
            pl.BlockSpec(bias.shape, lambda h: (0, 0, 0, 0, 0)),
            mine, mine, mine,
            pl.BlockSpec((3, own, HD), lambda h: (0, 0, first + h)),
            table, table,
        ] + specs,
        out_specs=[column, column, table, table] + extra_specs,
        scratch_shapes=[
            pltpu.VMEM((2 * own, HD), jnp.bfloat16),
            pltpu.VMEM((2 * own, HD), jnp.bfloat16),
            pltpu.VMEM((8, 2 * own), jnp.float32),
            pltpu.VMEM((2 * own, HD), jnp.bfloat16),
            pltpu.VMEM((count, HD), jnp.float32),
            pltpu.VMEM((count, HD), jnp.float32),
        ] + more,
        out_shape=[
            jax.ShapeDtypeStruct((own, width), jnp.bfloat16),
            jax.ShapeDtypeStruct((own, width), jnp.bfloat16),
            jax.ShapeDtypeStruct((count, width), jnp.bfloat16),
            jax.ShapeDtypeStruct((count, width), jnp.bfloat16),
        ] + extra,
        compiler_params=pltpu.CompilerParams(
            collective_id=1 if gathering else 2, has_side_effects=True,
            vmem_limit_bytes=56 * 2 ** 20,
        ),
        cost_estimate=pl.CostEstimate(
            flops=20 * own * count * width, bytes_accessed=14 * own * width + 8 * count * width,
            transcendentals=2 * own * count * heads,
        ),
    )(bias, q, g, o, swapped, keys, values, *moved)


def dequantize(codes, scales):
    count, length, width = codes.shape
    heads = scales.shape[2]
    values = (
        codes.astype(jnp.float32).reshape(count, length, heads, width // heads)
        * scales.astype(jnp.float32)[..., None]
    )
    return values.reshape(count, length, width).astype(jnp.bfloat16)


def swap(array):
    return lax.ppermute(array, "core", [(0, 1), (1, 0)])


def in_order(core, mine, other, axis):
    return jnp.where(
        core == 0,
        jnp.concatenate([mine, other], axis=axis),
        jnp.concatenate([other, mine], axis=axis),
    )


def on_device(group_count, lines, query, out_grad, forward_out, key_codes, key_scale, value_codes, value_scale, pairing):
    core = lax.axis_index("core")
    group = lax.axis_index("grp")
    blocks, tokens, width = query.shape
    half = width // 2
    own = blocks * tokens
    table = jnp.stack([dequantize(key_codes, key_scale), dequantize(value_codes, value_scale)])
    kept = lax.dynamic_slice_in_dim(table, core * half, half, axis=3)
    other = swap(lax.dynamic_slice_in_dim(table, (1 - core) * half, half, axis=3))
    shard = in_order(core, kept, other, 2)
    kv_local, kv_tokens = shard.shape[1:3]
    shard = shard.reshape(2, kv_local * kv_tokens, half)
    shards = [(shard[0, :, at:at + half // 2], shard[1, :, at:at + half // 2]) for at in (0, half // 2)]
    near = [a.reshape(-1, half // 2) for a in gather(*shards[0], lines)]
    flat = [a.reshape(own, width) for a in (query, out_grad, forward_out)]
    swapped = swap(jnp.stack([
        lax.dynamic_slice_in_dim(a, (1 - core) * half, half, axis=1) for a in flat
    ]))
    chips = near[0].shape[0] // (group_count * kv_local * kv_tokens)
    chosen = lax.dynamic_slice_in_dim(pairing, group * blocks, blocks, axis=0)
    hit = jnp.any(chosen[None] == jnp.arange(group_count * kv_local)[:, None, None], axis=2)
    bias = jnp.where(hit, 0.0, -jnp.inf).astype(jnp.float32)
    bias = jnp.tile(jnp.repeat(bias, tokens, axis=1), (1, 2))
    bias = bias.reshape(group_count, 1, kv_local, 1, 2 * own)
    bias = jnp.broadcast_to(bias, (group_count, chips, kv_local, 1, 2 * own))
    split = (2, lines, 2, kv_local * kv_tokens, half // 2)
    mine_0, other_0, dk_0, dv_0, *far = local_grads(
        0, 2, lines, bias, *flat, swapped, *near, shards[1], True
    )
    far = [a.reshape(-1, half // 2) for a in far]
    mine_1, other_1, dk_1, dv_1, sums_0 = local_grads(
        1, 2, lines, bias, *flat, swapped, *far, (dk_0.reshape(split), dv_0.reshape(split)), False
    )
    sums_1 = scatter(dk_1.reshape(split), dv_1.reshape(split))
    dq = in_order(
        core, jnp.concatenate([mine_0, mine_1], axis=1),
        jnp.concatenate([swap(other_0), swap(other_1)], axis=1), 1,
    ).reshape(query.shape)
    sums = jnp.concatenate([sums_0, sums_1], axis=2).reshape(2, kv_local, kv_tokens, half)
    length = kv_tokens // 2
    kept = lax.dynamic_slice_in_dim(sums, core * length, length, axis=2)
    other = swap(lax.dynamic_slice_in_dim(sums, (1 - core) * length, length, axis=2))
    grads = in_order(core, kept, other, 3)
    return dq, grads[0], grads[1]


def solution(mesh):
    groups, heads = mesh.shape["grp"], mesh.shape["head"]
    split = Mesh(mesh.devices.reshape(groups, heads // 2, 2), ("grp", "chip", "core"))
    spec = P("grp", ("chip", "core"), None)
    return jax.shard_map(
        functools.partial(on_device, groups, heads // 4),
        mesh=split,
        in_specs=(spec,) * 7 + (P(),),
        out_specs=(spec,) * 3,
        check_vma=False,
    )
```
